32 devices in a mesh: lead: 8 (over z, x), sub: 4 (over y, core).
Axes of the slice: x: 2, y: 2, z: 4, core: 2. Of those that a mesh axis runs over, the one named last changes fastest.
Arguments:
- state: float32 [67108864], P(('lead', 'sub')), may hold values from 0.135 to 67, as said below
- couplings: float32 [2, 16], replicated, may hold values from 0.25 to 16, as said below
Outputs:
- evolved: float32 [67108864], P(('lead', 'sub'))
- log_growth: float32 [], replicated
The draws below stay inside these ranges and needn't reach their ends.
Inputs may be any that keep to these rules, and one draw needn't show every extreme that they name: `state`: every entry is positive. `couplings`: row 0 lies between 8 and 16, row 1 between 0.25 and 0.5.
All inputs are finite; a program needn't handle non-finite values.
Results may differ from the reference program's by a relative error of at most 0.0003.
Values sent between devices are 32-bit elements; how exact they have to be, the bound alone decides.
A program may use at most 128 MiB of HBM per device.

```python
import jax
import jax.numpy as jnp
from jax import lax

W = 13
BLOCK = 4
WINDOWS = 2
SITES = 16


def draw_state(key, part):
    position = jnp.arange(4 ** W, dtype=jnp.int32)
    period = 4 ** (W - 2 * BLOCK)
    fraction = (position % period).astype(jnp.float32) / period
    jitter = jnp.clip(0.8 * jax.random.normal(key, (4 ** W,), jnp.float32), -2.0, 2.0)
    ramp_up = 1.0 + 4.0 * fraction
    return jnp.exp(jitter) * ramp_up


def draw_couplings(key, part):
    vertical_key = jax.random.fold_in(key, 11)
    horizontal_key = jax.random.fold_in(key, 23)
    vertical = jax.random.uniform(vertical_key, (SITES,), jnp.float32, 8.0, 16.0)
    horizontal = jax.random.uniform(horizontal_key, (SITES,), jnp.float32, 0.25, 0.5)
    return jnp.stack([vertical, horizontal])


def setup_inputs(seed: int = 0) -> dict:
    streams_of = jax.random.split(jax.random.key(seed), 3)
    state = draw_state(jax.random.fold_in(streams_of[2], 71), 0)
    couplings = draw_couplings(jax.random.fold_in(streams_of[2], 71), 0)
    return {"state": state, "couplings": couplings}


def one_site(field, vertical, horizontal):
    middle = field.shape[0] // 16
    shaped = field.reshape(4, middle, 4)
    summed = jnp.sum(shaped, axis=0)
    labels = jnp.arange(4, dtype=jnp.int32)

    def column(spin_value):
        spin_row = lax.dynamic_index_in_dim(shaped, spin_value, 0, keepdims=False)
        same_spin = (labels == spin_value).astype(field.dtype)
        return (summed + vertical * spin_row) * (1.0 + horizontal * same_spin)[None, :]

    columns = lax.map(column, labels)
    return jnp.transpose(columns, (1, 2, 0)).reshape(-1)


def reference(state, couplings):
    field_now = state
    growth = jnp.zeros((), state.dtype)
    for window in range(WINDOWS):
        for site_step in range(2 * BLOCK):
            site_index = window * 2 * BLOCK + site_step
            field_now = one_site(field_now, couplings[0, site_index], couplings[1, site_index])
        mean_value = jnp.sum(field_now) / field_now.shape[0]
        field_now = field_now / mean_value
        growth = growth + jnp.log(mean_value)
    return field_now, growth
```

```python
import jax
import jax.numpy as jnp
from jax import lax
from jax.experimental import pallas as pl
from jax.experimental.pallas import tpu as pltpu
from jax.sharding import PartitionSpec as P

BLOCK = 4
WINDOWS = 2


def block_kernel(vertical, horizontal, spread):
    position = jnp.arange(spread, dtype=jnp.int32)
    digits = [position // 4 ** (BLOCK - 1 - level) % 4 for level in range(BLOCK)]
    kernel = jnp.ones((spread, spread), jnp.float32)
    for level in range(BLOCK):
        same_spin = (digits[level][:, None] == digits[level][None, :]).astype(jnp.float32)
        kernel = kernel * (1.0 + vertical[level] * same_spin)
    for level in range(1, BLOCK):
        chained = (digits[level - 1] == digits[level]).astype(jnp.float32)
        kernel = kernel * (1.0 + horizontal[level] * chained)[None, :]
    labels = jnp.arange(4, dtype=jnp.int32)
    first_bond = 1.0 + horizontal[0] * (labels[:, None] == labels[None, :]).astype(jnp.float32)
    return (kernel, first_bond)


def multiply(matrix, kernel):
    return lax.dot_general(
        matrix,
        kernel,
        (((0,), (0,)), ((), ())),
        precision=lax.Precision.HIGHEST,
        preferred_element_type=jnp.float32,
    )


def bond_first(result, first_bond, spread):
    bonded = result.reshape(-1, 4, 4, spread // 4) * first_bond[None, :, :, None]
    return bonded.reshape(-1)


def contract_first(received, kernel, spread):
    item_count = received.shape[-1]
    return multiply(received.reshape(spread, -1, item_count), kernel)


def regroup(current, block_depth, kernel, first_bond, lead_count, sub_count, spread):
    devices = lead_count * sub_count
    span_rows = spread**block_depth
    low_rows = span_rows // devices
    rest_cols = current.shape[0] // span_rows
    shaped = current.reshape(1, low_rows, devices, rest_cols)
    result = contract_first(
        lax.all_to_all(shaped, ("lead", "sub"), split_axis=2, concat_axis=0, tiled=True),
        kernel,
        spread,
    )
    return bond_first(result, first_bond, spread)


def local_block(current, kernel, first_bond, spread):
    result = multiply(current.reshape(spread, -1), kernel)
    return bond_first(result, first_bond, spread)


def shards(state, couplings):
    lead_count = lax.axis_size("lead")
    sub_count = lax.axis_size("sub")
    devices = lead_count * sub_count
    spread = 4**BLOCK
    whole_count = state.shape[0] * devices
    period_blocks = 2
    current = state
    growth = jnp.zeros((), jnp.float32)
    for window in range(WINDOWS):
        for half_step in range(2):
            first_site = (2 * window + half_step) * BLOCK
            kernel, first_bond = block_kernel(
                couplings[0, first_site : first_site + BLOCK],
                couplings[1, first_site : first_site + BLOCK],
                spread,
            )
            if half_step % period_blocks == 0:
                current = regroup(
                    current, period_blocks, kernel, first_bond, lead_count, sub_count, spread
                )
            else:
                current = local_block(current, kernel, first_bond, spread)
        grand_total = lax.psum(jnp.sum(current), ("lead", "sub"))
        mean_value = grand_total / whole_count
        current = current / mean_value
        growth = growth + jnp.log(mean_value)
    return (current, growth)


MESH = pl.DeviceIdType.MESH
DEVICES = 32
CHUNKS = 4


def split(value):
    high = value.astype(jnp.bfloat16)
    return high, (value - high.astype(jnp.float32)).astype(jnp.bfloat16)


def dot3(left, right, dims):
    (lh, ll), (rh, rl) = left, right
    dot = lambda a, b: lax.dot_general(a, b, (dims, ((), ())), preferred_element_type=jnp.float32)
    return dot(lh, rh) + (dot(lh, rl) + dot(ll, rh))


def digit(index, place):
    return (index // 4**place) % 4


def partner(me, step):
    other = 0
    for bit in range(5):
        a, b = (me // 2**bit) % 2, (step // 2**bit) % 2
        other = other + (a + b - 2 * a * b) * 2**bit
    return other


def place_of(device):
    return (device // 4, device % 4)


def exchange_kernel(
    coup, x_hbm, u_hbm, total_ref,
    xin, sbuf, rbuf, stage, l_hi, l_lo, a_hi, a_lo, k_hi, k_lo, factor, part, gathered,
    in_sem, out_sem, own_sem, send_sem, recv_sem, sum_send, sum_recv,
):
    me = lax.axis_index("lead") * 4 + lax.axis_index("sub")
    d3, d4, d5_high = me // 8, (me // 2) % 4, me % 2

    def v(site):
        return coup[0, site]

    def h(site):
        return coup[1, site]

    loads = [
        pltpu.make_async_copy(x_hbm.at[half], xin.at[half], in_sem.at[half]) for half in range(2)
    ]
    for load in loads:
        load.start()

    barrier = pltpu.get_barrier_semaphore()

    @pl.loop(1, DEVICES)
    def _(step):
        pl.semaphore_signal(
            barrier, inc=1, device_id=place_of(partner(me, step)), device_id_type=MESH
        )

    pl.semaphore_wait(barrier, DEVICES - 1)

    def bond(site, one, other):
        return jnp.where(one == other, 1.0 + h(site), 1.0)

    def hop(site, one, other):
        return jnp.where(one == other, 1.0 + v(site), 1.0)

    rows = lax.broadcasted_iota(jnp.int32, (256, 256), 0)
    cols = lax.broadcasted_iota(jnp.int32, (256, 256), 1)
    a_mat = hop(5, digit(rows, 3), digit(cols, 3)) * hop(6, digit(rows, 2), digit(cols, 2))
    a_mat = a_mat * hop(7, digit(rows, 1), digit(cols, 1)) * hop(8, digit(rows, 0), digit(cols, 0))
    a_hi[...], a_lo[...] = split(a_mat)
    l_mat = hop(9, digit(rows, 3), digit(cols, 3)) * hop(10, digit(rows, 1), digit(cols, 2))
    l_mat = l_mat * hop(11, digit(rows, 0), digit(cols, 1))
    l_mat = jnp.where(digit(rows, 2) == digit(cols, 0), l_mat, 0.0)
    l_hi[...], l_lo[...] = split(l_mat)

    def copy_to(chunk, step):
        other = partner(me, step)
        return pltpu.make_async_remote_copy(
            src_ref=sbuf.at[chunk, other],
            dst_ref=rbuf.at[chunk, pl.ds(pl.multiple_of(me * 128, 128), 128)],
            send_sem=send_sem.at[chunk, step],
            recv_sem=recv_sem.at[chunk, step],
            device_id=place_of(other),
            device_id_type=MESH,
        )

    for load in loads:
        load.wait()

    for half in range(2):

        @pl.loop(0, 512, step=8)
        def _(row):
            where = pl.ds(pl.multiple_of(row, 8), 8)
            values = [xin[half, block, where, :] for block in range(16)]
            for site, stride in ((3, 4), (4, 1)):
                fresh = list(values)
                for first in range(16):
                    if (first // stride) % 4 == 0:
                        group = [first + stride * spin for spin in range(4)]
                        total = (values[group[0]] + values[group[1]]) + (
                            values[group[2]] + values[group[3]]
                        )
                        for member in group:
                            fresh[member] = total + v(site) * values[member]
                values = fresh
            for block in range(16):
                xin[half, block, where, :] = values[block]

    @pl.loop(0, 16)
    def _(count):
        step = 15 - count
        block = partner(me, 2 * step) // 2
        for half in range(2):
            view = xin.at[half, block]
            even = view[pl.ds(0, 256, stride=2), :]
            odd = view[pl.ds(1, 256, stride=2), :]
            pair = jnp.concatenate([even, odd], axis=1)
            lanes = dot3((l_hi[...], l_lo[...]), split(pair), ((1,), (1,)))
            result = dot3(split(lanes), (a_hi[...], a_lo[...]), ((1,), (0,)))
            for chunk in range(CHUNKS):
                for low in range(2):
                    sbuf[chunk, 2 * block + low, 64 * half : 64 * half + 64, :] = result[
                        64 * chunk : 64 * chunk + 64, 128 * low : 128 * low + 128
                    ]

        @pl.when(step > 0)
        def _():
            copy_to(0, 2 * step + 1).start()
            copy_to(0, 2 * step).start()

        @pl.when(step == 0)
        def _():
            copy_to(0, 1).start()

    def send_chunk(chunk):
        @pl.loop(0, DEVICES - 1)
        def _(count):
            copy_to(chunk, DEVICES - 1 - count).start()

    send_chunk(1)
    own = [
        pltpu.make_async_copy(
            sbuf.at[chunk, me],
            rbuf.at[chunk, pl.ds(pl.multiple_of(me * 128, 128), 128)],
            own_sem.at[chunk],
        )
        for chunk in range(CHUNKS)
    ]
    for copy in own:
        copy.start()

    rows = lax.broadcasted_iota(jnp.int32, (256, 128), 0)
    cols = lax.broadcasted_iota(jnp.int32, (256, 128), 1)
    e0, e1, e2 = digit(cols, 2), digit(cols, 1), digit(cols, 0)
    first = hop(0, digit(rows, 3), e0) * bond(0, digit(rows, 0), e0)
    first = first * hop(1, digit(rows, 2), e1) * bond(1, e0, e1)
    first = first * hop(2, digit(rows, 1), e2) * bond(2, e1, e2) * bond(3, e2, d3)
    first = jnp.where(cols < 64, first, 0.0)
    rows = lax.broadcasted_iota(jnp.int32, (128, 256), 0)
    cols = lax.broadcasted_iota(jnp.int32, (128, 256), 1)
    f0, f1, f2 = digit(cols, 2), digit(cols, 1), digit(cols, 0)
    last = hop(13, digit(rows, 2), f0) * bond(13, digit(cols, 3), f0)
    last = last * hop(14, digit(rows, 1), f1) * bond(14, f0, f1)
    last = last * hop(15, digit(rows, 0), f2) * bond(15, f1, f2)
    both = lax.dot_general(
        first, last, (((1,), (0,)), ((), ())),
        precision=lax.Precision.HIGHEST, preferred_element_type=jnp.float32,
    )
    rows = lax.broadcasted_iota(jnp.int32, (256, 256), 0)
    cols = lax.broadcasted_iota(jnp.int32, (256, 256), 1)
    both = both * hop(12, digit(rows, 0), digit(cols, 3))
    for d11 in range(4):
        k_hi[d11], k_lo[d11] = split(both * bond(12, d11, digit(cols, 3)))

    rows = lax.broadcasted_iota(jnp.int32, (64, 128), 0)
    cols = lax.broadcasted_iota(jnp.int32, (64, 128), 1)
    d5 = 2 * d5_high + cols // 64
    table = bond(5, d4, d5) * bond(6, d5, digit(cols, 2)) * bond(7, digit(cols, 2), digit(cols, 1))
    table = table * bond(8, digit(cols, 1), digit(cols, 0)) * bond(9, digit(cols, 0), digit(rows, 2))
    table = table * bond(10, digit(rows, 2), digit(rows, 1)) * bond(11, digit(rows, 1), digit(rows, 0))
    factor[...] = table * bond(4, d3 + 0 * cols, d4)
    part[...] = jnp.zeros_like(part)

    for copy in own:
        copy.wait()

    def store_of(chunk):
        return pltpu.make_async_copy(stage.at[chunk], u_hbm.at[:, chunk], out_sem.at[chunk])

    @pl.loop(0, CHUNKS)
    def _(chunk):
        @pl.loop(1, DEVICES)
        def _(step):
            copy_to(chunk, step).wait()

        @pl.when(chunk + 2 < CHUNKS)
        def _():
            send_chunk(chunk + 2)

        received = rbuf.at[chunk]

        for rest in range(16):
            values = received[pl.ds(rest, 256, stride=16), :]
            values = values * factor[pl.ds(chunk * 16 + rest, 1), :]
            turned = split(values.T)
            result = dot3(turned, (k_hi[rest % 4], k_lo[rest % 4]), ((1,), (0,)))
            for high in range(2):
                piece = result[:, 128 * high : 128 * high + 128]
                stage[chunk, :, 2 * rest + high, :] = piece
                part[...] += jnp.sum(piece.reshape(16, 8, 128), axis=0)
        store_of(chunk).start()

    gathered[pl.ds(me, 1)] = part[...][None]

    def sum_to(step):
        return pltpu.make_async_remote_copy(
            src_ref=part,
            dst_ref=gathered.at[me],
            send_sem=sum_send.at[step],
            recv_sem=sum_recv.at[step],
            device_id=place_of(partner(me, step)),
            device_id_type=MESH,
        )

    @pl.loop(1, DEVICES)
    def _(step):
        sum_to(step).start()

    @pl.loop(0, CHUNKS)
    def _(chunk):
        store_of(chunk).wait()

    @pl.loop(1, DEVICES)
    def _(step):
        sum_to(step).wait()

    total_ref[...] = jnp.sum(gathered[...], axis=0)


def exchanged(state, couplings):
    f32, bf16 = jnp.float32, jnp.bfloat16
    dma = pltpu.SemaphoreType.DMA
    unscaled, total = pl.pallas_call(
        exchange_kernel,
        out_shape=(
            jax.ShapeDtypeStruct((128, CHUNKS, 32, 128), f32),
            jax.ShapeDtypeStruct((8, 128), f32),
        ),
        in_specs=[pl.BlockSpec(memory_space=pltpu.SMEM), pl.BlockSpec(memory_space=pl.ANY)],
        out_specs=(pl.BlockSpec(memory_space=pl.ANY), pl.BlockSpec(memory_space=pltpu.VMEM)),
        scratch_shapes=[
            pltpu.VMEM((2, 16, 512, 128), f32),
            pltpu.VMEM((CHUNKS, DEVICES, 128, 128), f32),
            pltpu.VMEM((CHUNKS, 4096, 128), f32),
            pltpu.VMEM((CHUNKS, 128, 32, 128), f32),
            pltpu.VMEM((256, 256), bf16),
            pltpu.VMEM((256, 256), bf16),
            pltpu.VMEM((256, 256), bf16),
            pltpu.VMEM((256, 256), bf16),
            pltpu.VMEM((4, 256, 256), bf16),
            pltpu.VMEM((4, 256, 256), bf16),
            pltpu.VMEM((64, 128), f32),
            pltpu.VMEM((8, 128), f32),
            pltpu.VMEM((DEVICES, 8, 128), f32),
            dma((2,)),
            dma((CHUNKS,)),
            dma((CHUNKS,)),
            dma((CHUNKS, DEVICES)),
            dma((CHUNKS, DEVICES)),
            dma((DEVICES,)),
            dma((DEVICES,)),
        ],
        compiler_params=pltpu.CompilerParams(
            collective_id=0, has_side_effects=True, vmem_limit_bytes=48 * 2**20
        ),
    )(couplings, state.reshape(2, 16, 512, 128))
    mean_value = jnp.sum(total) / (state.shape[0] * DEVICES)
    return unscaled.reshape(-1) * (1.0 / mean_value), jnp.log(mean_value)


def solution(mesh):
    in_specs = (P(("lead", "sub")), P())
    out_specs = (P(("lead", "sub")), P())
    body = exchanged if dict(mesh.shape) == {"lead": 8, "sub": 4} else shards
    return jax.shard_map(body, mesh=mesh, in_specs=in_specs, out_specs=out_specs, check_vma=False)
```

```python
import jax
import jax.numpy as jnp
from jax import lax
from jax.experimental import pallas as pl
from jax.experimental.pallas import tpu as pltpu
from jax.sharding import PartitionSpec as P

BLOCK = 4
WINDOWS = 2


def block_kernel(vertical, horizontal, spread):
    position = jnp.arange(spread, dtype=jnp.int32)
    digits = [position // 4 ** (BLOCK - 1 - level) % 4 for level in range(BLOCK)]
    kernel = jnp.ones((spread, spread), jnp.float32)
    for level in range(BLOCK):
        same_spin = (digits[level][:, None] == digits[level][None, :]).astype(jnp.float32)
        kernel = kernel * (1.0 + vertical[level] * same_spin)
    for level in range(1, BLOCK):
        chained = (digits[level - 1] == digits[level]).astype(jnp.float32)
        kernel = kernel * (1.0 + horizontal[level] * chained)[None, :]
    labels = jnp.arange(4, dtype=jnp.int32)
    first_bond = 1.0 + horizontal[0] * (labels[:, None] == labels[None, :]).astype(jnp.float32)
    return (kernel, first_bond)


def multiply(matrix, kernel):
    return lax.dot_general(
        matrix,
        kernel,
        (((0,), (0,)), ((), ())),
        precision=lax.Precision.HIGHEST,
        preferred_element_type=jnp.float32,
    )


def bond_first(result, first_bond, spread):
    bonded = result.reshape(-1, 4, 4, spread // 4) * first_bond[None, :, :, None]
    return bonded.reshape(-1)


def contract_first(received, kernel, spread):
    item_count = received.shape[-1]
    return multiply(received.reshape(spread, -1, item_count), kernel)


def regroup(current, block_depth, kernel, first_bond, lead_count, sub_count, spread):
    devices = lead_count * sub_count
    span_rows = spread**block_depth
    low_rows = span_rows // devices
    rest_cols = current.shape[0] // span_rows
    shaped = current.reshape(1, low_rows, devices, rest_cols)
    result = contract_first(
        lax.all_to_all(shaped, ("lead", "sub"), split_axis=2, concat_axis=0, tiled=True),
        kernel,
        spread,
    )
    return bond_first(result, first_bond, spread)


def local_block(current, kernel, first_bond, spread):
    result = multiply(current.reshape(spread, -1), kernel)
    return bond_first(result, first_bond, spread)


def shards(state, couplings):
    lead_count = lax.axis_size("lead")
    sub_count = lax.axis_size("sub")
    devices = lead_count * sub_count
    spread = 4**BLOCK
    whole_count = state.shape[0] * devices
    period_blocks = 2
    current = state
    growth = jnp.zeros((), jnp.float32)
    for window in range(WINDOWS):
        for half_step in range(2):
            first_site = (2 * window + half_step) * BLOCK
            kernel, first_bond = block_kernel(
                couplings[0, first_site : first_site + BLOCK],
                couplings[1, first_site : first_site + BLOCK],
                spread,
            )
            if half_step % period_blocks == 0:
                current = regroup(
                    current, period_blocks, kernel, first_bond, lead_count, sub_count, spread
                )
            else:
                current = local_block(current, kernel, first_bond, spread)
        grand_total = lax.psum(jnp.sum(current), ("lead", "sub"))
        mean_value = grand_total / whole_count
        current = current / mean_value
        growth = growth + jnp.log(mean_value)
    return (current, growth)


MESH = pl.DeviceIdType.MESH
DEVICES = 32
CHUNKS = 4


def split(value):
    high = value.astype(jnp.bfloat16)
    return high, (value - high.astype(jnp.float32)).astype(jnp.bfloat16)


def dot3(left, right, dims):
    (lh, ll), (rh, rl) = left, right
    dot = lambda a, b: lax.dot_general(a, b, (dims, ((), ())), preferred_element_type=jnp.float32)
    return dot(lh, rh) + (dot(lh, rl) + dot(ll, rh))


def digit(index, place):
    return (index // 4**place) % 4


def partner(me, step):
    other = 0
    for bit in range(5):
        a, b = (me // 2**bit) % 2, (step // 2**bit) % 2
        other = other + (a + b - 2 * a * b) * 2**bit
    return other


def place_of(device):
    return (device // 4, device % 4)


def exchange_kernel(
    coup, x_hbm, u_ref, total_ref,
    xin, sbuf, rbuf, l_hi, l_lo, a_hi, a_lo, k_hi, k_lo, factor, part, gathered,
    in_sem, own_sem, send_sem, recv_sem, sum_send, sum_recv,
):
    me = lax.axis_index("lead") * 4 + lax.axis_index("sub")
    d3, d4, d5_high = me // 8, (me // 2) % 4, me % 2

    def v(site):
        return coup[0, site]

    def h(site):
        return coup[1, site]

    loads = [
        pltpu.make_async_copy(x_hbm.at[half], xin.at[half], in_sem.at[half]) for half in range(2)
    ]
    for load in loads:
        load.start()

    barrier = pltpu.get_barrier_semaphore()

    @pl.loop(1, DEVICES)
    def _(step):
        pl.semaphore_signal(
            barrier, inc=1, device_id=place_of(partner(me, step)), device_id_type=MESH
        )

    def bond(site, one, other):
        return jnp.where(one == other, 1.0 + h(site), 1.0)

    def hop(site, one, other):
        return jnp.where(one == other, 1.0 + v(site), 1.0)

    rows = lax.broadcasted_iota(jnp.int32, (256, 256), 0)
    cols = lax.broadcasted_iota(jnp.int32, (256, 256), 1)
    a_mat = hop(5, digit(rows, 3), digit(cols, 3)) * hop(6, digit(rows, 2), digit(cols, 2))
    a_mat = a_mat * hop(7, digit(rows, 1), digit(cols, 1)) * hop(8, digit(rows, 0), digit(cols, 0))
    a_hi[...], a_lo[...] = split(a_mat)
    l_mat = hop(9, digit(rows, 3), digit(cols, 3)) * hop(10, digit(rows, 1), digit(cols, 2))
    l_mat = l_mat * hop(11, digit(rows, 0), digit(cols, 1))
    l_mat = jnp.where(digit(rows, 2) == digit(cols, 0), l_mat, 0.0)
    l_hi[...], l_lo[...] = split(l_mat)

    def copy_to(chunk, step):
        other = partner(me, step)
        return pltpu.make_async_remote_copy(
            src_ref=sbuf.at[chunk, other],
            dst_ref=rbuf.at[chunk, pl.ds(pl.multiple_of(me * 128, 128), 128)],
            send_sem=send_sem.at[chunk, step],
            recv_sem=recv_sem.at[chunk, step],
            device_id=place_of(other),
            device_id_type=MESH,
        )

    for load in loads:
        load.wait()

    for half in range(2):

        @pl.loop(0, 512, step=8)
        def _(row):
            where = pl.ds(pl.multiple_of(row, 8), 8)
            values = [xin[half, block, where, :] for block in range(16)]
            for site, stride in ((3, 4), (4, 1)):
                fresh = list(values)
                for first in range(16):
                    if (first // stride) % 4 == 0:
                        group = [first + stride * spin for spin in range(4)]
                        total = (values[group[0]] + values[group[1]]) + (
                            values[group[2]] + values[group[3]]
                        )
                        for member in group:
                            fresh[member] = total + v(site) * values[member]
                values = fresh
            for block in range(16):
                xin[half, block, where, :] = values[block]

    pl.semaphore_wait(barrier, DEVICES - 1)

    @pl.loop(0, 16)
    def _(count):
        step = 15 - count // 2 - 8 * (count % 2)
        block = partner(me, 2 * step) // 2
        for half in range(2):
            view = xin.at[half, block]
            even = view[pl.ds(0, 256, stride=2), :]
            odd = view[pl.ds(1, 256, stride=2), :]
            pair = jnp.concatenate([even, odd], axis=1)
            lanes = dot3((l_hi[...], l_lo[...]), split(pair), ((1,), (1,)))
            result = dot3(split(lanes), (a_hi[...], a_lo[...]), ((1,), (0,)))
            for chunk in range(CHUNKS):
                for low in range(2):
                    sbuf[chunk, 2 * block + low, 64 * half : 64 * half + 64, :] = result[
                        64 * chunk : 64 * chunk + 64, 128 * low : 128 * low + 128
                    ]

        @pl.when(step > 0)
        def _():
            copy_to(0, 2 * step + 1).start()
            copy_to(0, 2 * step).start()

        @pl.when(step == 0)
        def _():
            copy_to(0, 1).start()

    def send_chunk(chunk):
        @pl.loop(0, DEVICES - 1)
        def _(count):
            copy_to(chunk, DEVICES - 1 - count // 2 - 16 * (count % 2)).start()

    send_chunk(1)
    own = [
        pltpu.make_async_copy(
            sbuf.at[chunk, me],
            rbuf.at[chunk, pl.ds(pl.multiple_of(me * 128, 128), 128)],
            own_sem.at[chunk],
        )
        for chunk in range(CHUNKS)
    ]
    for copy in own:
        copy.start()

    rows = lax.broadcasted_iota(jnp.int32, (256, 128), 0)
    cols = lax.broadcasted_iota(jnp.int32, (256, 128), 1)
    e0, e1, e2 = digit(cols, 2), digit(cols, 1), digit(cols, 0)
    first = hop(0, digit(rows, 3), e0) * bond(0, digit(rows, 0), e0)
    first = first * hop(1, digit(rows, 2), e1) * bond(1, e0, e1)
    first = first * hop(2, digit(rows, 1), e2) * bond(2, e1, e2) * bond(3, e2, d3)
    first = jnp.where(cols < 64, first, 0.0)
    rows = lax.broadcasted_iota(jnp.int32, (128, 256), 0)
    cols = lax.broadcasted_iota(jnp.int32, (128, 256), 1)
    f0, f1, f2 = digit(cols, 2), digit(cols, 1), digit(cols, 0)
    last = hop(13, digit(rows, 2), f0) * bond(13, digit(cols, 3), f0)
    last = last * hop(14, digit(rows, 1), f1) * bond(14, f0, f1)
    last = last * hop(15, digit(rows, 0), f2) * bond(15, f1, f2)
    both = lax.dot_general(
        first, last, (((1,), (0,)), ((), ())),
        precision=lax.Precision.HIGHEST, preferred_element_type=jnp.float32,
    )
    rows = lax.broadcasted_iota(jnp.int32, (256, 256), 0)
    cols = lax.broadcasted_iota(jnp.int32, (256, 256), 1)
    both = both * hop(12, digit(rows, 0), digit(cols, 3))
    for d11 in range(4):
        k_hi[d11], k_lo[d11] = split(both * bond(12, d11, digit(cols, 3)))

    rows = lax.broadcasted_iota(jnp.int32, (64, 128), 0)
    cols = lax.broadcasted_iota(jnp.int32, (64, 128), 1)
    d5 = 2 * d5_high + cols // 64
    table = bond(5, d4, d5) * bond(6, d5, digit(cols, 2)) * bond(7, digit(cols, 2), digit(cols, 1))
    table = table * bond(8, digit(cols, 1), digit(cols, 0)) * bond(9, digit(cols, 0), digit(rows, 2))
    table = table * bond(10, digit(rows, 2), digit(rows, 1)) * bond(11, digit(rows, 1), digit(rows, 0))
    factor[...] = table * bond(4, d3 + 0 * cols, d4)
    part[...] = jnp.zeros_like(part)

    for copy in own:
        copy.wait()

    @pl.loop(0, CHUNKS)
    def _(chunk):
        @pl.loop(1, DEVICES)
        def _(step):
            copy_to(chunk, step).wait()

        @pl.when(chunk + 2 < CHUNKS)
        def _():
            send_chunk(chunk + 2)

        received = rbuf.at[chunk]

        for d11 in range(4):
            turned = []
            for d10 in range(4):
                rest = 4 * d10 + d11
                values = received[pl.ds(rest, 256, stride=16), :]
                values = values * factor[pl.ds(chunk * 16 + rest, 1), :]
                turned.append(values.T)
            turned = split(jnp.concatenate(turned, axis=0))
            result = dot3(turned, (k_hi[d11], k_lo[d11]), ((1,), (0,)))
            part[...] += jnp.sum(
                (result[:, :128] + result[:, 128:]).reshape(64, 8, 128), axis=0
            )
            for d10 in range(4):
                for high in range(2):
                    u_ref[:, chunk, 8 * d10 + 2 * d11 + high, :] = result[
                        128 * d10 : 128 * d10 + 128, 128 * high : 128 * high + 128
                    ]

    gathered[pl.ds(me, 1)] = part[...][None]

    def sum_to(step):
        return pltpu.make_async_remote_copy(
            src_ref=part,
            dst_ref=gathered.at[me],
            send_sem=sum_send.at[step],
            recv_sem=sum_recv.at[step],
            device_id=place_of(partner(me, step)),
            device_id_type=MESH,
        )

    @pl.loop(1, DEVICES)
    def _(step):
        sum_to(step).start()

    @pl.loop(1, DEVICES)
    def _(step):
        sum_to(step).wait()

    total_ref[...] = jnp.sum(gathered[...], axis=0)


def exchanged(state, couplings):
    f32, bf16 = jnp.float32, jnp.bfloat16
    dma = pltpu.SemaphoreType.DMA
    unscaled, total = pl.pallas_call(
        exchange_kernel,
        out_shape=(
            jax.ShapeDtypeStruct((128, CHUNKS, 32, 128), f32),
            jax.ShapeDtypeStruct((8, 128), f32),
        ),
        in_specs=[pl.BlockSpec(memory_space=pltpu.SMEM), pl.BlockSpec(memory_space=pl.ANY)],
        out_specs=(pl.BlockSpec(memory_space=pltpu.VMEM),) * 2,
        scratch_shapes=[
            pltpu.VMEM((2, 16, 512, 128), f32),
            pltpu.VMEM((CHUNKS, DEVICES, 128, 128), f32),
            pltpu.VMEM((CHUNKS, 4096, 128), f32),
            pltpu.VMEM((256, 256), bf16),
            pltpu.VMEM((256, 256), bf16),
            pltpu.VMEM((256, 256), bf16),
            pltpu.VMEM((256, 256), bf16),
            pltpu.VMEM((4, 256, 256), bf16),
            pltpu.VMEM((4, 256, 256), bf16),
            pltpu.VMEM((64, 128), f32),
            pltpu.VMEM((8, 128), f32),
            pltpu.VMEM((DEVICES, 8, 128), f32),
            dma((2,)),
            dma((CHUNKS,)),
            dma((CHUNKS, DEVICES)),
            dma((CHUNKS, DEVICES)),
            dma((DEVICES,)),
            dma((DEVICES,)),
        ],
        compiler_params=pltpu.CompilerParams(
            collective_id=0, has_side_effects=True, vmem_limit_bytes=40 * 2**20
        ),
    )(couplings, state.reshape(2, 16, 512, 128))
    mean_value = jnp.sum(total) / (state.shape[0] * DEVICES)
    return unscaled.reshape(-1) * (1.0 / mean_value), jnp.log(mean_value)


def solution(mesh):
    in_specs = (P(("lead", "sub")), P())
    out_specs = (P(("lead", "sub")), P())
    body = exchanged if dict(mesh.shape) == {"lead": 8, "sub": 4} else shards
    return jax.shard_map(body, mesh=mesh, in_specs=in_specs, out_specs=out_specs, check_vma=False)
```

```python
import functools

import jax
import jax.numpy as jnp
from jax import lax
from jax.experimental import pallas as pl
from jax.experimental.pallas import tpu as pltpu
from jax.sharding import PartitionSpec as P

BLOCK = 4
WINDOWS = 2


def block_kernel(vertical, horizontal, spread):
    position = jnp.arange(spread, dtype=jnp.int32)
    digits = [position // 4 ** (BLOCK - 1 - level) % 4 for level in range(BLOCK)]
    kernel = jnp.ones((spread, spread), jnp.float32)
    for level in range(BLOCK):
        same_spin = (digits[level][:, None] == digits[level][None, :]).astype(jnp.float32)
        kernel = kernel * (1.0 + vertical[level] * same_spin)
    for level in range(1, BLOCK):
        chained = (digits[level - 1] == digits[level]).astype(jnp.float32)
        kernel = kernel * (1.0 + horizontal[level] * chained)[None, :]
    labels = jnp.arange(4, dtype=jnp.int32)
    first_bond = 1.0 + horizontal[0] * (labels[:, None] == labels[None, :]).astype(jnp.float32)
    return (kernel, first_bond)


def multiply(matrix, kernel):
    return lax.dot_general(
        matrix,
        kernel,
        (((0,), (0,)), ((), ())),
        precision=lax.Precision.HIGHEST,
        preferred_element_type=jnp.float32,
    )


def bond_first(result, first_bond, spread):
    bonded = result.reshape(-1, 4, 4, spread // 4) * first_bond[None, :, :, None]
    return bonded.reshape(-1)


def contract_first(received, kernel, spread):
    item_count = received.shape[-1]
    return multiply(received.reshape(spread, -1, item_count), kernel)


def regroup(current, block_depth, kernel, first_bond, lead_count, sub_count, spread):
    devices = lead_count * sub_count
    span_rows = spread**block_depth
    low_rows = span_rows // devices
    rest_cols = current.shape[0] // span_rows
    shaped = current.reshape(1, low_rows, devices, rest_cols)
    result = contract_first(
        lax.all_to_all(shaped, ("lead", "sub"), split_axis=2, concat_axis=0, tiled=True),
        kernel,
        spread,
    )
    return bond_first(result, first_bond, spread)


def local_block(current, kernel, first_bond, spread):
    result = multiply(current.reshape(spread, -1), kernel)
    return bond_first(result, first_bond, spread)


def shards(state, couplings):
    lead_count = lax.axis_size("lead")
    sub_count = lax.axis_size("sub")
    devices = lead_count * sub_count
    spread = 4**BLOCK
    whole_count = state.shape[0] * devices
    period_blocks = 2
    current = state
    growth = jnp.zeros((), jnp.float32)
    for window in range(WINDOWS):
        for half_step in range(2):
            first_site = (2 * window + half_step) * BLOCK
            kernel, first_bond = block_kernel(
                couplings[0, first_site : first_site + BLOCK],
                couplings[1, first_site : first_site + BLOCK],
                spread,
            )
            if half_step % period_blocks == 0:
                current = regroup(
                    current, period_blocks, kernel, first_bond, lead_count, sub_count, spread
                )
            else:
                current = local_block(current, kernel, first_bond, spread)
        grand_total = lax.psum(jnp.sum(current), ("lead", "sub"))
        mean_value = grand_total / whole_count
        current = current / mean_value
        growth = growth + jnp.log(mean_value)
    return (current, growth)


MESH = pl.DeviceIdType.MESH
DEVICES = 32
CHUNKS = 4
PARTS = 16


def split(value):
    high = value.astype(jnp.bfloat16)
    return high, (value - high.astype(jnp.float32)).astype(jnp.bfloat16)


def dot3(left, right, dims):
    (lh, ll), (rh, rl) = left, right
    dot = lambda a, b: lax.dot_general(a, b, (dims, ((), ())), preferred_element_type=jnp.float32)
    return dot(lh, rh) + (dot(lh, rl) + dot(ll, rh))


def digit(index, place):
    return (index // 4**place) % 4


def partner(me, step):
    other = 0
    for bit in range(5):
        a, b = (me // 2**bit) % 2, (step // 2**bit) % 2
        other = other + (a + b - 2 * a * b) * 2**bit
    return other


def place_of(device):
    return (device // 4, device % 4)


def exchange_kernel(
    coup, x_hbm, u_ref, total_ref,
    xin, sbuf, rbuf, l_hi, l_lo, a_hi, a_lo, k_hi, k_lo, factor, part, gathered,
    in_sem, own_sem, send_sem, recv_sem, sum_send, sum_recv,
):
    me = lax.axis_index("lead") * 4 + lax.axis_index("sub")
    d3, d4, d5_high = me // 8, (me // 2) % 4, me % 2

    def v(site):
        return coup[0, site]

    def h(site):
        return coup[1, site]

    loads = [
        pltpu.make_async_copy(x_hbm.at[half], xin.at[half], in_sem.at[half]) for half in range(2)
    ]
    for load in loads:
        load.start()

    barrier = pltpu.get_barrier_semaphore()

    @pl.loop(1, DEVICES)
    def _(step):
        pl.semaphore_signal(
            barrier, inc=1, device_id=place_of(partner(me, step)), device_id_type=MESH
        )

    def bond(site, one, other):
        return jnp.where(one == other, 1.0 + h(site), 1.0)

    def hop(site, one, other):
        return jnp.where(one == other, 1.0 + v(site), 1.0)

    rows = lax.broadcasted_iota(jnp.int32, (256, 256), 0)
    cols = lax.broadcasted_iota(jnp.int32, (256, 256), 1)
    a_mat = hop(5, digit(rows, 3), digit(cols, 3)) * hop(6, digit(rows, 2), digit(cols, 2))
    a_mat = a_mat * hop(7, digit(rows, 1), digit(cols, 1)) * hop(8, digit(rows, 0), digit(cols, 0))
    a_hi[...], a_lo[...] = split(a_mat)
    l_mat = hop(9, digit(rows, 3), digit(cols, 3)) * hop(10, digit(rows, 1), digit(cols, 2))
    l_mat = l_mat * hop(11, digit(rows, 0), digit(cols, 1))
    l_mat = jnp.where(digit(rows, 2) == digit(cols, 0), l_mat, 0.0)
    l_hi[...], l_lo[...] = split(l_mat)

    def copy_to(chunk, step):
        other = partner(me, step)
        return pltpu.make_async_remote_copy(
            src_ref=sbuf.at[chunk, other],
            dst_ref=rbuf.at[chunk, pl.ds(pl.multiple_of(me * 128, 128), 128)],
            send_sem=send_sem.at[chunk, step],
            recv_sem=recv_sem.at[chunk, step],
            device_id=place_of(other),
            device_id_type=MESH,
        )

    for load in loads:
        load.wait()

    for half in range(2):

        @pl.loop(0, 512, step=8)
        def _(row):
            where = pl.ds(pl.multiple_of(row, 8), 8)
            values = [xin[half, block, where, :] for block in range(16)]
            for site, stride in ((3, 4), (4, 1)):
                fresh = list(values)
                for first in range(16):
                    if (first // stride) % 4 == 0:
                        group = [first + stride * spin for spin in range(4)]
                        total = (values[group[0]] + values[group[1]]) + (
                            values[group[2]] + values[group[3]]
                        )
                        for member in group:
                            fresh[member] = total + v(site) * values[member]
                values = fresh
            for block in range(16):
                xin[half, block, where, :] = values[block]

    pl.semaphore_wait(barrier, DEVICES - 1)

    @pl.loop(0, 16)
    def _(count):
        step = 15 - count // 2 - 8 * (count % 2)
        block = partner(me, 2 * step) // 2
        for half in range(2):
            view = xin.at[half, block]
            even = view[pl.ds(0, 256, stride=2), :]
            odd = view[pl.ds(1, 256, stride=2), :]
            pair = jnp.concatenate([even, odd], axis=1)
            lanes = dot3((l_hi[...], l_lo[...]), split(pair), ((1,), (1,)))
            result = dot3(split(lanes), (a_hi[...], a_lo[...]), ((1,), (0,)))
            for chunk in range(CHUNKS):
                for low in range(2):
                    sbuf[chunk, 2 * block + low, 64 * half : 64 * half + 64, :] = result[
                        64 * chunk : 64 * chunk + 64, 128 * low : 128 * low + 128
                    ]

        @pl.when(step > 0)
        def _():
            copy_to(0, 2 * step + 1).start()
            copy_to(0, 2 * step).start()

        @pl.when(step == 0)
        def _():
            copy_to(0, 1).start()

    def send_chunk(chunk):
        @pl.loop(0, DEVICES - 1)
        def _(count):
            copy_to(chunk, DEVICES - 1 - count // 2 - 16 * (count % 2)).start()

    for chunk in range(1, CHUNKS):
        send_chunk(chunk)
    own = [
        pltpu.make_async_copy(
            sbuf.at[chunk, me],
            rbuf.at[chunk, pl.ds(pl.multiple_of(me * 128, 128), 128)],
            own_sem.at[chunk],
        )
        for chunk in range(CHUNKS)
    ]
    for copy in own:
        copy.start()

    rows = lax.broadcasted_iota(jnp.int32, (256, 128), 0)
    cols = lax.broadcasted_iota(jnp.int32, (256, 128), 1)
    e0, e1, e2 = digit(cols, 2), digit(cols, 1), digit(cols, 0)
    first = hop(0, digit(rows, 3), e0) * bond(0, digit(rows, 0), e0)
    first = first * hop(1, digit(rows, 2), e1) * bond(1, e0, e1)
    first = first * hop(2, digit(rows, 1), e2) * bond(2, e1, e2) * bond(3, e2, d3)
    first = jnp.where(cols < 64, first, 0.0)
    rows = lax.broadcasted_iota(jnp.int32, (128, 256), 0)
    cols = lax.broadcasted_iota(jnp.int32, (128, 256), 1)
    f0, f1, f2 = digit(cols, 2), digit(cols, 1), digit(cols, 0)
    last = hop(13, digit(rows, 2), f0) * bond(13, digit(cols, 3), f0)
    last = last * hop(14, digit(rows, 1), f1) * bond(14, f0, f1)
    last = last * hop(15, digit(rows, 0), f2) * bond(15, f1, f2)
    both = lax.dot_general(
        first, last, (((1,), (0,)), ((), ())),
        precision=lax.Precision.HIGHEST, preferred_element_type=jnp.float32,
    )
    rows = lax.broadcasted_iota(jnp.int32, (256, 256), 0)
    cols = lax.broadcasted_iota(jnp.int32, (256, 256), 1)
    both = both * hop(12, digit(rows, 0), digit(cols, 3))
    for d11 in range(4):
        k_hi[d11], k_lo[d11] = split(both * bond(12, d11, digit(cols, 3)))

    rows = lax.broadcasted_iota(jnp.int32, (64, 128), 0)
    cols = lax.broadcasted_iota(jnp.int32, (64, 128), 1)
    d5 = 2 * d5_high + cols // 64
    table = bond(5, d4, d5) * bond(6, d5, digit(cols, 2)) * bond(7, digit(cols, 2), digit(cols, 1))
    table = table * bond(8, digit(cols, 1), digit(cols, 0)) * bond(9, digit(cols, 0), digit(rows, 2))
    table = table * bond(10, digit(rows, 2), digit(rows, 1)) * bond(11, digit(rows, 1), digit(rows, 0))
    factor[...] = table * bond(4, d3 + 0 * cols, d4)
    part[...] = jnp.zeros_like(part)

    for copy in own:
        copy.wait()

    @pl.loop(0, CHUNKS)
    def _(chunk):
        @pl.loop(1, DEVICES)
        def _(step):
            copy_to(chunk, step).wait()

        received = rbuf.at[chunk]

        for d11 in range(4):
            turned = []
            for d10 in range(4):
                rest = 4 * d10 + d11
                values = received[pl.ds(rest, 256, stride=16), :]
                values = values * factor[pl.ds(chunk * 16 + rest, 1), :]
                turned.append(values.T)
            turned = split(jnp.concatenate(turned, axis=0))
            result = dot3(turned, (k_hi[d11], k_lo[d11]), ((1,), (0,)))
            part[...] += jnp.sum(
                (result[:, :128] + result[:, 128:]).reshape(64, 8, 128), axis=0
            )
            for d10 in range(4):
                for high in range(2):
                    u_ref[:, chunk, 8 * d10 + 2 * d11 + high, :] = result[
                        128 * d10 : 128 * d10 + 128, 128 * high : 128 * high + 128
                    ]

    gathered[pl.ds(me, 1)] = part[...][None]

    def sum_to(step):
        return pltpu.make_async_remote_copy(
            src_ref=part,
            dst_ref=gathered.at[me],
            send_sem=sum_send.at[step],
            recv_sem=sum_recv.at[step],
            device_id=place_of(partner(me, step)),
            device_id_type=MESH,
        )

    @pl.loop(1, DEVICES)
    def _(step):
        sum_to(step).start()

    @pl.loop(1, DEVICES)
    def _(step):
        sum_to(step).wait()

    total_ref[...] = jnp.sum(gathered[...], axis=0)


def scale_kernel(whole_count, u_ref, total_ref, out_hbm, growth_ref, stage, sem):
    mean_value = jnp.sum(total_ref[...], keepdims=True) / whole_count
    growth_ref[...] = jnp.log(mean_value)
    scale = 1.0 / mean_value

    def store_of(part):
        return pltpu.make_async_copy(stage.at[part], out_hbm.at[part], sem.at[part])

    @pl.loop(0, PARTS)
    def _(part):
        stage[part] = u_ref[part] * scale
        store_of(part).start()

    @pl.loop(0, PARTS)
    def _(part):
        store_of(part).wait()


def exchanged(state, couplings):
    f32, bf16 = jnp.float32, jnp.bfloat16
    dma = pltpu.SemaphoreType.DMA
    unscaled, total = pl.pallas_call(
        exchange_kernel,
        out_shape=(
            jax.ShapeDtypeStruct((128, CHUNKS, 32, 128), f32),
            jax.ShapeDtypeStruct((8, 128), f32),
        ),
        in_specs=[pl.BlockSpec(memory_space=pltpu.SMEM), pl.BlockSpec(memory_space=pl.ANY)],
        out_specs=(pl.BlockSpec(memory_space=pltpu.VMEM),) * 2,
        scratch_shapes=[
            pltpu.VMEM((2, 16, 512, 128), f32),
            pltpu.VMEM((CHUNKS, DEVICES, 128, 128), f32),
            pltpu.VMEM((CHUNKS, 4096, 128), f32),
            pltpu.VMEM((256, 256), bf16),
            pltpu.VMEM((256, 256), bf16),
            pltpu.VMEM((256, 256), bf16),
            pltpu.VMEM((256, 256), bf16),
            pltpu.VMEM((4, 256, 256), bf16),
            pltpu.VMEM((4, 256, 256), bf16),
            pltpu.VMEM((64, 128), f32),
            pltpu.VMEM((8, 128), f32),
            pltpu.VMEM((DEVICES, 8, 128), f32),
            dma((2,)),
            dma((CHUNKS,)),
            dma((CHUNKS, DEVICES)),
            dma((CHUNKS, DEVICES)),
            dma((DEVICES,)),
            dma((DEVICES,)),
        ],
        compiler_params=pltpu.CompilerParams(
            collective_id=0, has_side_effects=True, vmem_limit_bytes=40 * 2**20
        ),
    )(couplings, state.reshape(2, 16, 512, 128))
    rows = state.shape[0] // (128 * PARTS)
    evolved, growth = pl.pallas_call(
        functools.partial(scale_kernel, state.shape[0] * DEVICES),
        out_shape=(
            jax.ShapeDtypeStruct((PARTS, rows, 128), f32),
            jax.ShapeDtypeStruct((1, 1), f32),
        ),
        in_specs=[pl.BlockSpec(memory_space=pltpu.VMEM)] * 2,
        out_specs=(pl.BlockSpec(memory_space=pl.ANY), pl.BlockSpec(memory_space=pltpu.VMEM)),
        scratch_shapes=[pltpu.VMEM((PARTS, rows, 128), f32), dma((PARTS,))],
        compiler_params=pltpu.CompilerParams(vmem_limit_bytes=24 * 2**20),
    )(unscaled.reshape(PARTS, rows, 128), total)
    return evolved.reshape(-1), growth.reshape(())


def solution(mesh):
    in_specs = (P(("lead", "sub")), P())
    out_specs = (P(("lead", "sub")), P())
    body = exchanged if dict(mesh.shape) == {"lead": 8, "sub": 4} else shards
    return jax.shard_map(body, mesh=mesh, in_specs=in_specs, out_specs=out_specs, check_vma=False)
```

```python
import functools

import jax
import jax.numpy as jnp
from jax import lax
from jax.experimental import pallas as pl
from jax.experimental.pallas import tpu as pltpu
from jax.sharding import PartitionSpec as P

BLOCK = 4
WINDOWS = 2


def block_kernel(vertical, horizontal, spread):
    position = jnp.arange(spread, dtype=jnp.int32)
    digits = [position // 4 ** (BLOCK - 1 - level) % 4 for level in range(BLOCK)]
    kernel = jnp.ones((spread, spread), jnp.float32)
    for level in range(BLOCK):
        same_spin = (digits[level][:, None] == digits[level][None, :]).astype(jnp.float32)
        kernel = kernel * (1.0 + vertical[level] * same_spin)
    for level in range(1, BLOCK):
        chained = (digits[level - 1] == digits[level]).astype(jnp.float32)
        kernel = kernel * (1.0 + horizontal[level] * chained)[None, :]
    labels = jnp.arange(4, dtype=jnp.int32)
    first_bond = 1.0 + horizontal[0] * (labels[:, None] == labels[None, :]).astype(jnp.float32)
    return (kernel, first_bond)


def multiply(matrix, kernel):
    return lax.dot_general(
        matrix,
        kernel,
        (((0,), (0,)), ((), ())),
        precision=lax.Precision.HIGHEST,
        preferred_element_type=jnp.float32,
    )


def bond_first(result, first_bond, spread):
    bonded = result.reshape(-1, 4, 4, spread // 4) * first_bond[None, :, :, None]
    return bonded.reshape(-1)


def contract_first(received, kernel, spread):
    item_count = received.shape[-1]
    return multiply(received.reshape(spread, -1, item_count), kernel)


def regroup(current, block_depth, kernel, first_bond, lead_count, sub_count, spread):
    devices = lead_count * sub_count
    span_rows = spread**block_depth
    low_rows = span_rows // devices
    rest_cols = current.shape[0] // span_rows
    shaped = current.reshape(1, low_rows, devices, rest_cols)
    result = contract_first(
        lax.all_to_all(shaped, ("lead", "sub"), split_axis=2, concat_axis=0, tiled=True),
        kernel,
        spread,
    )
    return bond_first(result, first_bond, spread)


def local_block(current, kernel, first_bond, spread):
    result = multiply(current.reshape(spread, -1), kernel)
    return bond_first(result, first_bond, spread)


def shards(state, couplings):
    lead_count = lax.axis_size("lead")
    sub_count = lax.axis_size("sub")
    devices = lead_count * sub_count
    spread = 4**BLOCK
    whole_count = state.shape[0] * devices
    period_blocks = 2
    current = state
    growth = jnp.zeros((), jnp.float32)
    for window in range(WINDOWS):
        for half_step in range(2):
            first_site = (2 * window + half_step) * BLOCK
            kernel, first_bond = block_kernel(
                couplings[0, first_site : first_site + BLOCK],
                couplings[1, first_site : first_site + BLOCK],
                spread,
            )
            if half_step % period_blocks == 0:
                current = regroup(
                    current, period_blocks, kernel, first_bond, lead_count, sub_count, spread
                )
            else:
                current = local_block(current, kernel, first_bond, spread)
        grand_total = lax.psum(jnp.sum(current), ("lead", "sub"))
        mean_value = grand_total / whole_count
        current = current / mean_value
        growth = growth + jnp.log(mean_value)
    return (current, growth)


MESH = pl.DeviceIdType.MESH
DEVICES = 32
CHUNKS = 4
PARTS = 16


def split(value):
    high = value.astype(jnp.bfloat16)
    return high, (value - high.astype(jnp.float32)).astype(jnp.bfloat16)


def dot3(left, right, dims):
    (lh, ll), (rh, rl) = left, right
    dot = lambda a, b: lax.dot_general(a, b, (dims, ((), ())), preferred_element_type=jnp.float32)
    return dot(lh, rh) + (dot(lh, rl) + dot(ll, rh))


def digit(index, place):
    return (index // 4**place) % 4


def partner(me, step, bits=5):
    other = 0
    for bit in range(bits):
        a, b = (me // 2**bit) % 2, (step // 2**bit) % 2
        other = other + (a + b - 2 * a * b) * 2**bit
    return other


def place_of(device):
    return (device // 4, device % 4)


def exchange_kernel(
    coup, x_hbm, u_ref, total_ref,
    xin, sbuf, abuf, rbuf, l_hi, l_lo, a_hi, a_lo, k_hi, k_lo, factor, part, gathered,
    in_sem, own_sem, a_send, a_recv, b_send, b_recv, sum_send, sum_recv,
):
    me = lax.axis_index("lead") * 4 + lax.axis_index("sub")
    d3, d4, d5_high = me // 8, (me // 2) % 4, me % 2
    plane, spot = me // 8, me % 8

    def v(site):
        return coup[0, site]

    def h(site):
        return coup[1, site]

    loads = [
        pltpu.make_async_copy(x_hbm.at[half], xin.at[half], in_sem.at[half]) for half in range(2)
    ]
    for load in loads:
        load.start()

    barrier = pltpu.get_barrier_semaphore()

    @pl.loop(1, DEVICES)
    def _(step):
        pl.semaphore_signal(
            barrier, inc=1, device_id=place_of(partner(me, step)), device_id_type=MESH
        )

    def bond(site, one, other):
        return jnp.where(one == other, 1.0 + h(site), 1.0)

    def hop(site, one, other):
        return jnp.where(one == other, 1.0 + v(site), 1.0)

    rows = lax.broadcasted_iota(jnp.int32, (256, 256), 0)
    cols = lax.broadcasted_iota(jnp.int32, (256, 256), 1)
    a_mat = hop(5, digit(rows, 3), digit(cols, 3)) * hop(6, digit(rows, 2), digit(cols, 2))
    a_mat = a_mat * hop(7, digit(rows, 1), digit(cols, 1)) * hop(8, digit(rows, 0), digit(cols, 0))
    a_hi[...], a_lo[...] = split(a_mat)
    l_mat = hop(9, digit(rows, 3), digit(cols, 3)) * hop(10, digit(rows, 1), digit(cols, 2))
    l_mat = l_mat * hop(11, digit(rows, 0), digit(cols, 1))
    l_mat = jnp.where(digit(rows, 2) == digit(cols, 0), l_mat, 0.0)
    l_hi[...], l_lo[...] = split(l_mat)

    def received_from(source):
        return pl.ds(pl.multiple_of(source * 128, 128), 128)

    def within(chunk, turn, hop):
        there, target = partner(spot, hop, 3), partner(plane, turn, 2)
        return pltpu.make_async_remote_copy(
            src_ref=sbuf.at[chunk, 8 * target + there],
            dst_ref=abuf.at[chunk, turn, spot],
            send_sem=a_send.at[chunk, turn, hop],
            recv_sem=a_recv.at[chunk, turn, hop],
            device_id=place_of(8 * plane + there),
            device_id_type=MESH,
        )

    def settle(chunk, hop):
        there = partner(spot, hop, 3)
        return pltpu.make_async_remote_copy(
            src_ref=sbuf.at[chunk, 8 * plane + there],
            dst_ref=rbuf.at[chunk, received_from(me)],
            send_sem=a_send.at[chunk, 0, hop],
            recv_sem=a_recv.at[chunk, 0, hop],
            device_id=place_of(8 * plane + there),
            device_id_type=MESH,
        )

    def across(chunk, turn, hop, source=None):
        origin, target = partner(spot, hop, 3), partner(plane, turn, 2)
        return pltpu.make_async_remote_copy(
            src_ref=abuf.at[chunk, turn, origin] if source is None else source,
            dst_ref=rbuf.at[chunk, received_from(8 * plane + origin)],
            send_sem=b_send.at[chunk, turn, hop],
            recv_sem=b_recv.at[chunk, turn, hop],
            device_id=place_of(8 * target + spot),
            device_id_type=MESH,
        )

    def across_own(chunk, turn):
        target = partner(plane, turn, 2)
        return across(chunk, turn, 0, sbuf.at[chunk, 8 * target + spot])

    def depart(chunk, count):
        turn, half = 3 - count // 4, 3 - count % 4

        @pl.when(turn > 0)
        def _():
            within(chunk, turn, 2 * half + 1).start()

            @pl.when(half > 0)
            def _():
                within(chunk, turn, 2 * half).start()

            @pl.when(half == 0)
            def _():
                across_own(chunk, turn).start()

        @pl.when(turn == 0)
        def _():
            settle(chunk, 2 * half + 1).start()

            @pl.when(half > 0)
            def _():
                settle(chunk, 2 * half).start()

    def depart_all(chunk):
        @pl.loop(0, 16)
        def _(count):
            depart(chunk, count)

    def forward(chunk):
        @pl.loop(0, 3)
        def _(count):
            turn = 3 - count

            @pl.loop(1, 8)
            def _(hop):
                within(chunk, turn, 8 - hop).wait_recv()
                across(chunk, turn, 8 - hop).start()

    for load in loads:
        load.wait()

    for half in range(2):

        @pl.loop(0, 512, step=8)
        def _(row):
            where = pl.ds(pl.multiple_of(row, 8), 8)
            values = [xin[half, block, where, :] for block in range(16)]
            for site, stride in ((3, 4), (4, 1)):
                fresh = list(values)
                for first in range(16):
                    if (first // stride) % 4 == 0:
                        group = [first + stride * spin for spin in range(4)]
                        total = (values[group[0]] + values[group[1]]) + (
                            values[group[2]] + values[group[3]]
                        )
                        for member in group:
                            fresh[member] = total + v(site) * values[member]
                values = fresh
            for block in range(16):
                xin[half, block, where, :] = values[block]

    pl.semaphore_wait(barrier, DEVICES - 1)

    @pl.loop(0, 16)
    def _(count):
        block = partner(me // 2, 15 - count, 4)
        for half in range(2):
            view = xin.at[half, block]
            even = view[pl.ds(0, 256, stride=2), :]
            odd = view[pl.ds(1, 256, stride=2), :]
            pair = jnp.concatenate([even, odd], axis=1)
            lanes = dot3((l_hi[...], l_lo[...]), split(pair), ((1,), (1,)))
            result = dot3(split(lanes), (a_hi[...], a_lo[...]), ((1,), (0,)))
            for chunk in range(CHUNKS):
                for low in range(2):
                    sbuf[chunk, 2 * block + low, 64 * half : 64 * half + 64, :] = result[
                        64 * chunk : 64 * chunk + 64, 128 * low : 128 * low + 128
                    ]

        depart(0, count)

    depart_all(1)
    forward(0)
    depart_all(2)
    own = [
        pltpu.make_async_copy(
            sbuf.at[chunk, me],
            rbuf.at[chunk, pl.ds(pl.multiple_of(me * 128, 128), 128)],
            own_sem.at[chunk],
        )
        for chunk in range(CHUNKS)
    ]
    for copy in own:
        copy.start()

    rows = lax.broadcasted_iota(jnp.int32, (256, 128), 0)
    cols = lax.broadcasted_iota(jnp.int32, (256, 128), 1)
    e0, e1, e2 = digit(cols, 2), digit(cols, 1), digit(cols, 0)
    first = hop(0, digit(rows, 3), e0) * bond(0, digit(rows, 0), e0)
    first = first * hop(1, digit(rows, 2), e1) * bond(1, e0, e1)
    first = first * hop(2, digit(rows, 1), e2) * bond(2, e1, e2) * bond(3, e2, d3)
    first = jnp.where(cols < 64, first, 0.0)
    rows = lax.broadcasted_iota(jnp.int32, (128, 256), 0)
    cols = lax.broadcasted_iota(jnp.int32, (128, 256), 1)
    f0, f1, f2 = digit(cols, 2), digit(cols, 1), digit(cols, 0)
    last = hop(13, digit(rows, 2), f0) * bond(13, digit(cols, 3), f0)
    last = last * hop(14, digit(rows, 1), f1) * bond(14, f0, f1)
    last = last * hop(15, digit(rows, 0), f2) * bond(15, f1, f2)
    both = lax.dot_general(
        first, last, (((1,), (0,)), ((), ())),
        precision=lax.Precision.HIGHEST, preferred_element_type=jnp.float32,
    )
    rows = lax.broadcasted_iota(jnp.int32, (256, 256), 0)
    cols = lax.broadcasted_iota(jnp.int32, (256, 256), 1)
    both = both * hop(12, digit(rows, 0), digit(cols, 3))
    for d11 in range(4):
        k_hi[d11], k_lo[d11] = split(both * bond(12, d11, digit(cols, 3)))

    rows = lax.broadcasted_iota(jnp.int32, (64, 128), 0)
    cols = lax.broadcasted_iota(jnp.int32, (64, 128), 1)
    d5 = 2 * d5_high + cols // 64
    table = bond(5, d4, d5) * bond(6, d5, digit(cols, 2)) * bond(7, digit(cols, 2), digit(cols, 1))
    table = table * bond(8, digit(cols, 1), digit(cols, 0)) * bond(9, digit(cols, 0), digit(rows, 2))
    table = table * bond(10, digit(rows, 2), digit(rows, 1)) * bond(11, digit(rows, 1), digit(rows, 0))
    factor[...] = table * bond(4, d3 + 0 * cols, d4)
    part[...] = jnp.zeros_like(part)

    for copy in own:
        copy.wait()

    forward(1)
    depart_all(3)
    forward(2)
    forward(3)

    @pl.loop(0, CHUNKS)
    def _(chunk):
        @pl.loop(1, 8)
        def _(hop):
            settle(chunk, hop).wait()

        @pl.loop(0, 3)
        def _(count):
            @pl.loop(0, 8)
            def _(hop):
                across(chunk, 3 - count, hop).wait()

            @pl.loop(1, 8)
            def _(hop):
                within(chunk, 3 - count, hop).wait_send()

        received = rbuf.at[chunk]

        for d11 in range(4):
            turned = []
            for d10 in range(4):
                rest = 4 * d10 + d11
                values = received[pl.ds(rest, 256, stride=16), :]
                values = values * factor[pl.ds(chunk * 16 + rest, 1), :]
                turned.append(values.T)
            turned = split(jnp.concatenate(turned, axis=0))
            result = dot3(turned, (k_hi[d11], k_lo[d11]), ((1,), (0,)))
            part[...] += jnp.sum(
                (result[:, :128] + result[:, 128:]).reshape(64, 8, 128), axis=0
            )
            for d10 in range(4):
                for high in range(2):
                    u_ref[:, chunk, 8 * d10 + 2 * d11 + high, :] = result[
                        128 * d10 : 128 * d10 + 128, 128 * high : 128 * high + 128
                    ]

    gathered[pl.ds(me, 1)] = part[...][None]

    def sum_to(step):
        return pltpu.make_async_remote_copy(
            src_ref=part,
            dst_ref=gathered.at[me],
            send_sem=sum_send.at[step],
            recv_sem=sum_recv.at[step],
            device_id=place_of(partner(me, step)),
            device_id_type=MESH,
        )

    @pl.loop(1, DEVICES)
    def _(step):
        sum_to(step).start()

    @pl.loop(1, DEVICES)
    def _(step):
        sum_to(step).wait()

    total_ref[...] = jnp.sum(gathered[...], axis=0)


def scale_kernel(whole_count, u_ref, total_ref, out_hbm, growth_ref, stage, sem):
    mean_value = jnp.sum(total_ref[...], keepdims=True) / whole_count
    growth_ref[...] = jnp.log(mean_value)
    scale = 1.0 / mean_value

    def store_of(part):
        return pltpu.make_async_copy(stage.at[part], out_hbm.at[part], sem.at[part])

    @pl.loop(0, PARTS)
    def _(part):
        stage[part] = u_ref[part] * scale
        store_of(part).start()

    @pl.loop(0, PARTS)
    def _(part):
        store_of(part).wait()


def exchanged(state, couplings):
    f32, bf16 = jnp.float32, jnp.bfloat16
    dma = pltpu.SemaphoreType.DMA
    unscaled, total = pl.pallas_call(
        exchange_kernel,
        out_shape=(
            jax.ShapeDtypeStruct((128, CHUNKS, 32, 128), f32),
            jax.ShapeDtypeStruct((8, 128), f32),
        ),
        in_specs=[pl.BlockSpec(memory_space=pltpu.SMEM), pl.BlockSpec(memory_space=pl.ANY)],
        out_specs=(pl.BlockSpec(memory_space=pltpu.VMEM),) * 2,
        scratch_shapes=[
            pltpu.VMEM((2, 16, 512, 128), f32),
            pltpu.VMEM((CHUNKS, DEVICES, 128, 128), f32),
            pltpu.VMEM((CHUNKS, 4, 8, 128, 128), f32),
            pltpu.VMEM((CHUNKS, 4096, 128), f32),
            pltpu.VMEM((256, 256), bf16),
            pltpu.VMEM((256, 256), bf16),
            pltpu.VMEM((256, 256), bf16),
            pltpu.VMEM((256, 256), bf16),
            pltpu.VMEM((4, 256, 256), bf16),
            pltpu.VMEM((4, 256, 256), bf16),
            pltpu.VMEM((64, 128), f32),
            pltpu.VMEM((8, 128), f32),
            pltpu.VMEM((DEVICES, 8, 128), f32),
            dma((2,)),
            dma((CHUNKS,)),
            dma((CHUNKS, 4, 8)),
            dma((CHUNKS, 4, 8)),
            dma((CHUNKS, 4, 8)),
            dma((CHUNKS, 4, 8)),
            dma((DEVICES,)),
            dma((DEVICES,)),
        ],
        compiler_params=pltpu.CompilerParams(
            collective_id=0, has_side_effects=True, vmem_limit_bytes=44 * 2**20
        ),
    )(couplings, state.reshape(2, 16, 512, 128))
    rows = state.shape[0] // (128 * PARTS)
    evolved, growth = pl.pallas_call(
        functools.partial(scale_kernel, state.shape[0] * DEVICES),
        out_shape=(
            jax.ShapeDtypeStruct((PARTS, rows, 128), f32),
            jax.ShapeDtypeStruct((1, 1), f32),
        ),
        in_specs=[pl.BlockSpec(memory_space=pltpu.VMEM)] * 2,
        out_specs=(pl.BlockSpec(memory_space=pl.ANY), pl.BlockSpec(memory_space=pltpu.VMEM)),
        scratch_shapes=[pltpu.VMEM((PARTS, rows, 128), f32), dma((PARTS,))],
        compiler_params=pltpu.CompilerParams(vmem_limit_bytes=24 * 2**20),
    )(unscaled.reshape(PARTS, rows, 128), total)
    return evolved.reshape(-1), growth.reshape(())


def solution(mesh):
    in_specs = (P(("lead", "sub")), P())
    out_specs = (P(("lead", "sub")), P())
    body = exchanged if dict(mesh.shape) == {"lead": 8, "sub": 4} else shards
    return jax.shard_map(body, mesh=mesh, in_specs=in_specs, out_specs=out_specs, check_vma=False)
```

```python
import functools

import jax
import jax.numpy as jnp
from jax import lax
from jax.experimental import pallas as pl
from jax.experimental.pallas import tpu as pltpu
from jax.sharding import PartitionSpec as P

BLOCK = 4
WINDOWS = 2


def block_kernel(vertical, horizontal, spread):
    position = jnp.arange(spread, dtype=jnp.int32)
    digits = [position // 4 ** (BLOCK - 1 - level) % 4 for level in range(BLOCK)]
    kernel = jnp.ones((spread, spread), jnp.float32)
    for level in range(BLOCK):
        same_spin = (digits[level][:, None] == digits[level][None, :]).astype(jnp.float32)
        kernel = kernel * (1.0 + vertical[level] * same_spin)
    for level in range(1, BLOCK):
        chained = (digits[level - 1] == digits[level]).astype(jnp.float32)
        kernel = kernel * (1.0 + horizontal[level] * chained)[None, :]
    labels = jnp.arange(4, dtype=jnp.int32)
    first_bond = 1.0 + horizontal[0] * (labels[:, None] == labels[None, :]).astype(jnp.float32)
    return (kernel, first_bond)


def multiply(matrix, kernel):
    return lax.dot_general(
        matrix,
        kernel,
        (((0,), (0,)), ((), ())),
        precision=lax.Precision.HIGHEST,
        preferred_element_type=jnp.float32,
    )


def bond_first(result, first_bond, spread):
    bonded = result.reshape(-1, 4, 4, spread // 4) * first_bond[None, :, :, None]
    return bonded.reshape(-1)


def contract_first(received, kernel, spread):
    item_count = received.shape[-1]
    return multiply(received.reshape(spread, -1, item_count), kernel)


def regroup(current, block_depth, kernel, first_bond, lead_count, sub_count, spread):
    devices = lead_count * sub_count
    span_rows = spread**block_depth
    low_rows = span_rows // devices
    rest_cols = current.shape[0] // span_rows
    shaped = current.reshape(1, low_rows, devices, rest_cols)
    result = contract_first(
        lax.all_to_all(shaped, ("lead", "sub"), split_axis=2, concat_axis=0, tiled=True),
        kernel,
        spread,
    )
    return bond_first(result, first_bond, spread)


def local_block(current, kernel, first_bond, spread):
    result = multiply(current.reshape(spread, -1), kernel)
    return bond_first(result, first_bond, spread)


def shards(state, couplings):
    lead_count = lax.axis_size("lead")
    sub_count = lax.axis_size("sub")
    devices = lead_count * sub_count
    spread = 4**BLOCK
    whole_count = state.shape[0] * devices
    period_blocks = 2
    current = state
    growth = jnp.zeros((), jnp.float32)
    for window in range(WINDOWS):
        for half_step in range(2):
            first_site = (2 * window + half_step) * BLOCK
            kernel, first_bond = block_kernel(
                couplings[0, first_site : first_site + BLOCK],
                couplings[1, first_site : first_site + BLOCK],
                spread,
            )
            if half_step % period_blocks == 0:
                current = regroup(
                    current, period_blocks, kernel, first_bond, lead_count, sub_count, spread
                )
            else:
                current = local_block(current, kernel, first_bond, spread)
        grand_total = lax.psum(jnp.sum(current), ("lead", "sub"))
        mean_value = grand_total / whole_count
        current = current / mean_value
        growth = growth + jnp.log(mean_value)
    return (current, growth)


MESH = pl.DeviceIdType.MESH
DEVICES = 32
CHUNKS = 4
PARTS = 16
WINDOW = 16


def split(value):
    high = value.astype(jnp.bfloat16)
    return high, (value - high.astype(jnp.float32)).astype(jnp.bfloat16)


def dot3(left, right, dims):
    (lh, ll), (rh, rl) = left, right
    dot = lambda a, b: lax.dot_general(a, b, (dims, ((), ())), preferred_element_type=jnp.float32)
    return dot(lh, rh) + (dot(lh, rl) + dot(ll, rh))


def digit(index, place):
    return (index // 4**place) % 4


def partner(me, step):
    other = 0
    for bit in range(5):
        a, b = (me // 2**bit) % 2, (step // 2**bit) % 2
        other = other + (a + b - 2 * a * b) * 2**bit
    return other


def place_of(device):
    return (device // 4, device % 4)


def exchange_kernel(
    coup, x_hbm, u_ref, total_ref,
    xin, sbuf, rbuf, l_hi, l_lo, a_hi, a_lo, k_hi, k_lo, factor, part, gathered,
    in_sem, own_sem, send_sem, recv_sem, sum_send, sum_recv,
):
    me = lax.axis_index("lead") * 4 + lax.axis_index("sub")
    d3, d4, d5_high = me // 8, (me // 2) % 4, me % 2

    def v(site):
        return coup[0, site]

    def h(site):
        return coup[1, site]

    loads = [
        pltpu.make_async_copy(x_hbm.at[half], xin.at[half], in_sem.at[half]) for half in range(2)
    ]
    for load in loads:
        load.start()

    barrier = pltpu.get_barrier_semaphore()

    @pl.loop(1, DEVICES)
    def _(step):
        pl.semaphore_signal(
            barrier, inc=1, device_id=place_of(partner(me, step)), device_id_type=MESH
        )

    def bond(site, one, other):
        return jnp.where(one == other, 1.0 + h(site), 1.0)

    def hop(site, one, other):
        return jnp.where(one == other, 1.0 + v(site), 1.0)

    rows = lax.broadcasted_iota(jnp.int32, (256, 256), 0)
    cols = lax.broadcasted_iota(jnp.int32, (256, 256), 1)
    a_mat = hop(5, digit(rows, 3), digit(cols, 3)) * hop(6, digit(rows, 2), digit(cols, 2))
    a_mat = a_mat * hop(7, digit(rows, 1), digit(cols, 1)) * hop(8, digit(rows, 0), digit(cols, 0))
    a_hi[...], a_lo[...] = split(a_mat)
    l_mat = hop(9, digit(rows, 3), digit(cols, 3)) * hop(10, digit(rows, 1), digit(cols, 2))
    l_mat = l_mat * hop(11, digit(rows, 0), digit(cols, 1))
    l_mat = jnp.where(digit(rows, 2) == digit(cols, 0), l_mat, 0.0)
    l_hi[...], l_lo[...] = split(l_mat)

    def copy_to(chunk, step):
        other = partner(me, step)
        return pltpu.make_async_remote_copy(
            src_ref=sbuf.at[chunk, other],
            dst_ref=rbuf.at[chunk, pl.ds(pl.multiple_of(me * 128, 128), 128)],
            send_sem=send_sem.at[chunk, step],
            recv_sem=recv_sem.at[chunk, step],
            device_id=place_of(other),
            device_id_type=MESH,
        )

    for load in loads:
        load.wait()

    for half in range(2):

        @pl.loop(0, 512, step=8)
        def _(row):
            where = pl.ds(pl.multiple_of(row, 8), 8)
            values = [xin[half, block, where, :] for block in range(16)]
            for site, stride in ((3, 4), (4, 1)):
                fresh = list(values)
                for first in range(16):
                    if (first // stride) % 4 == 0:
                        group = [first + stride * spin for spin in range(4)]
                        total = (values[group[0]] + values[group[1]]) + (
                            values[group[2]] + values[group[3]]
                        )
                        for member in group:
                            fresh[member] = total + v(site) * values[member]
                values = fresh
            for block in range(16):
                xin[half, block, where, :] = values[block]

    pl.semaphore_wait(barrier, DEVICES - 1)

    @pl.loop(0, 16)
    def _(count):
        step = 15 - count // 2 - 8 * (count % 2)
        block = partner(me, 2 * step) // 2
        for half in range(2):
            view = xin.at[half, block]
            even = view[pl.ds(0, 256, stride=2), :]
            odd = view[pl.ds(1, 256, stride=2), :]
            pair = jnp.concatenate([even, odd], axis=1)
            lanes = dot3((l_hi[...], l_lo[...]), split(pair), ((1,), (1,)))
            result = dot3(split(lanes), (a_hi[...], a_lo[...]), ((1,), (0,)))
            for chunk in range(CHUNKS):
                for low in range(2):
                    sbuf[chunk, 2 * block + low, 64 * half : 64 * half + 64, :] = result[
                        64 * chunk : 64 * chunk + 64, 128 * low : 128 * low + 128
                    ]

        @pl.when(step > 0)
        def _():
            copy_to(0, 2 * step + 1).start()
            copy_to(0, 2 * step).start()

        @pl.when(step == 0)
        def _():
            copy_to(0, 1).start()

    def numbered(number):
        count = number % (DEVICES - 1)
        return copy_to(number // (DEVICES - 1), DEVICES - 1 - count // 2 - 16 * (count % 2))

    def send_chunk(chunk):
        @pl.loop(chunk * (DEVICES - 1), (chunk + 1) * (DEVICES - 1))
        def _(number):
            numbered(number - WINDOW).wait_send()
            numbered(number).start()

    own = [
        pltpu.make_async_copy(
            sbuf.at[chunk, me],
            rbuf.at[chunk, pl.ds(pl.multiple_of(me * 128, 128), 128)],
            own_sem.at[chunk],
        )
        for chunk in range(CHUNKS)
    ]
    for copy in own:
        copy.start()

    rows = lax.broadcasted_iota(jnp.int32, (256, 128), 0)
    cols = lax.broadcasted_iota(jnp.int32, (256, 128), 1)
    e0, e1, e2 = digit(cols, 2), digit(cols, 1), digit(cols, 0)
    first = hop(0, digit(rows, 3), e0) * bond(0, digit(rows, 0), e0)
    first = first * hop(1, digit(rows, 2), e1) * bond(1, e0, e1)
    first = first * hop(2, digit(rows, 1), e2) * bond(2, e1, e2) * bond(3, e2, d3)
    first = jnp.where(cols < 64, first, 0.0)
    rows = lax.broadcasted_iota(jnp.int32, (128, 256), 0)
    cols = lax.broadcasted_iota(jnp.int32, (128, 256), 1)
    f0, f1, f2 = digit(cols, 2), digit(cols, 1), digit(cols, 0)
    last = hop(13, digit(rows, 2), f0) * bond(13, digit(cols, 3), f0)
    last = last * hop(14, digit(rows, 1), f1) * bond(14, f0, f1)
    last = last * hop(15, digit(rows, 0), f2) * bond(15, f1, f2)
    both = lax.dot_general(
        first, last, (((1,), (0,)), ((), ())),
        precision=lax.Precision.HIGHEST, preferred_element_type=jnp.float32,
    )
    rows = lax.broadcasted_iota(jnp.int32, (256, 256), 0)
    cols = lax.broadcasted_iota(jnp.int32, (256, 256), 1)
    both = both * hop(12, digit(rows, 0), digit(cols, 3))
    for d11 in range(4):
        k_hi[d11], k_lo[d11] = split(both * bond(12, d11, digit(cols, 3)))

    rows = lax.broadcasted_iota(jnp.int32, (64, 128), 0)
    cols = lax.broadcasted_iota(jnp.int32, (64, 128), 1)
    d5 = 2 * d5_high + cols // 64
    table = bond(5, d4, d5) * bond(6, d5, digit(cols, 2)) * bond(7, digit(cols, 2), digit(cols, 1))
    table = table * bond(8, digit(cols, 1), digit(cols, 0)) * bond(9, digit(cols, 0), digit(rows, 2))
    table = table * bond(10, digit(rows, 2), digit(rows, 1)) * bond(11, digit(rows, 1), digit(rows, 0))
    factor[...] = table * bond(4, d3 + 0 * cols, d4)
    part[...] = jnp.zeros_like(part)

    for copy in own:
        copy.wait()

    @pl.loop(0, DEVICES - 1 - WINDOW)
    def _(number):
        numbered(number).wait_send()

    send_chunk(1)
    send_chunk(2)

    @pl.loop(0, CHUNKS)
    def _(chunk):
        @pl.loop(1, DEVICES)
        def _(step):
            copy_to(chunk, step).wait_recv()

        received = rbuf.at[chunk]

        for d11 in range(4):
            turned = []
            for d10 in range(4):
                rest = 4 * d10 + d11
                values = received[pl.ds(rest, 256, stride=16), :]
                values = values * factor[pl.ds(chunk * 16 + rest, 1), :]
                turned.append(values.T)
            turned = split(jnp.concatenate(turned, axis=0))
            result = dot3(turned, (k_hi[d11], k_lo[d11]), ((1,), (0,)))
            part[...] += jnp.sum(
                (result[:, :128] + result[:, 128:]).reshape(64, 8, 128), axis=0
            )
            for d10 in range(4):
                for high in range(2):
                    u_ref[:, chunk, 8 * d10 + 2 * d11 + high, :] = result[
                        128 * d10 : 128 * d10 + 128, 128 * high : 128 * high + 128
                    ]

        @pl.when(chunk == 0)
        def _():
            send_chunk(3)

    @pl.loop(CHUNKS * (DEVICES - 1) - WINDOW, CHUNKS * (DEVICES - 1))
    def _(number):
        numbered(number).wait_send()

    gathered[pl.ds(me, 1)] = part[...][None]

    def sum_to(step):
        return pltpu.make_async_remote_copy(
            src_ref=part,
            dst_ref=gathered.at[me],
            send_sem=sum_send.at[step],
            recv_sem=sum_recv.at[step],
            device_id=place_of(partner(me, step)),
            device_id_type=MESH,
        )

    @pl.loop(1, DEVICES)
    def _(step):
        sum_to(step).start()

    @pl.loop(1, DEVICES)
    def _(step):
        sum_to(step).wait()

    total_ref[...] = jnp.sum(gathered[...], axis=0)


def scale_kernel(whole_count, u_ref, total_ref, out_hbm, growth_ref, stage, sem):
    mean_value = jnp.sum(total_ref[...], keepdims=True) / whole_count
    growth_ref[...] = jnp.log(mean_value)
    scale = 1.0 / mean_value

    def store_of(part):
        return pltpu.make_async_copy(stage.at[part], out_hbm.at[part], sem.at[part])

    @pl.loop(0, PARTS)
    def _(part):
        stage[part] = u_ref[part] * scale
        store_of(part).start()

    @pl.loop(0, PARTS)
    def _(part):
        store_of(part).wait()


def exchanged(state, couplings):
    f32, bf16 = jnp.float32, jnp.bfloat16
    dma = pltpu.SemaphoreType.DMA
    unscaled, total = pl.pallas_call(
        exchange_kernel,
        out_shape=(
            jax.ShapeDtypeStruct((128, CHUNKS, 32, 128), f32),
            jax.ShapeDtypeStruct((8, 128), f32),
        ),
        in_specs=[pl.BlockSpec(memory_space=pltpu.SMEM), pl.BlockSpec(memory_space=pl.ANY)],
        out_specs=(pl.BlockSpec(memory_space=pltpu.VMEM),) * 2,
        scratch_shapes=[
            pltpu.VMEM((2, 16, 512, 128), f32),
            pltpu.VMEM((CHUNKS, DEVICES, 128, 128), f32),
            pltpu.VMEM((CHUNKS, 4096, 128), f32),
            pltpu.VMEM((256, 256), bf16),
            pltpu.VMEM((256, 256), bf16),
            pltpu.VMEM((256, 256), bf16),
            pltpu.VMEM((256, 256), bf16),
            pltpu.VMEM((4, 256, 256), bf16),
            pltpu.VMEM((4, 256, 256), bf16),
            pltpu.VMEM((64, 128), f32),
            pltpu.VMEM((8, 128), f32),
            pltpu.VMEM((DEVICES, 8, 128), f32),
            dma((2,)),
            dma((CHUNKS,)),
            dma((CHUNKS, DEVICES)),
            dma((CHUNKS, DEVICES)),
            dma((DEVICES,)),
            dma((DEVICES,)),
        ],
        compiler_params=pltpu.CompilerParams(
            collective_id=0, has_side_effects=True, vmem_limit_bytes=40 * 2**20
        ),
    )(couplings, state.reshape(2, 16, 512, 128))
    rows = state.shape[0] // (128 * PARTS)
    evolved, growth = pl.pallas_call(
        functools.partial(scale_kernel, state.shape[0] * DEVICES),
        out_shape=(
            jax.ShapeDtypeStruct((PARTS, rows, 128), f32),
            jax.ShapeDtypeStruct((1, 1), f32),
        ),
        in_specs=[pl.BlockSpec(memory_space=pltpu.VMEM)] * 2,
        out_specs=(pl.BlockSpec(memory_space=pl.ANY), pl.BlockSpec(memory_space=pltpu.VMEM)),
        scratch_shapes=[pltpu.VMEM((PARTS, rows, 128), f32), dma((PARTS,))],
        compiler_params=pltpu.CompilerParams(vmem_limit_bytes=24 * 2**20),
    )(unscaled.reshape(PARTS, rows, 128), total)
    return evolved.reshape(-1), growth.reshape(())


def solution(mesh):
    in_specs = (P(("lead", "sub")), P())
    out_specs = (P(("lead", "sub")), P())
    body = exchanged if dict(mesh.shape) == {"lead": 8, "sub": 4} else shards
    return jax.shard_map(body, mesh=mesh, in_specs=in_specs, out_specs=out_specs, check_vma=False)
```
